512 devices in a mesh: row: 16 (over z), col: 32 (over x, y, core).
Axes of the slice: x: 4, y: 4, z: 16, core: 2. Of those that a mesh axis runs over, the one named last changes fastest.
Arguments:
- coords: float32 [3, 65536], P(None, ('row', 'col')), may hold values from -1 to 1
- residual_in: float32 [65536, 512], P(('row', 'col')), may hold values from -6 to 6
- link_mask: int32 [512, 2], P(('row', 'col')), may hold values 0 or 1
- compress: float32 [65536, 256], P(('row', 'col')), may hold values from -0.5 to 0.5
- expand: float32 [65536, 256], P(('row', 'col')), may hold values from -0.375 to 0.375
- level_gain: float32 [512, 1280], P(('row', 'col')), may hold values from 0.5 to 1.5
- level_couple: float32 [131072, 1280], P(('row', 'col')), may hold values from -0.1875 to 0.1875
- partner_perm: int32 [512, 5, 256], P(('row', 'col')), may hold values from 0 to 255, each once within a row
Outputs:
- new_residual: float32 [65536, 512], P(('row', 'col'))
- res_norms: float32 [512], replicated
The draws below stay inside these ranges and needn't reach their ends.
Inputs may be any that keep to these rules, and one draw needn't show every extreme that they name: `partner_perm`: each row of 256 entries names every number once.
All inputs are finite; a program needn't handle non-finite values. No bound on the sum of `link_mask` on one device may be relied on, other than what follows from the above.
Results may differ from the reference program's by a relative error of at most 0.0003.
Values sent between devices are 32-bit elements; how exact they have to be, the bound alone decides.
No kernel may reach another device: no remote copies, remote signals or barrier semaphores. Data moves between devices by JAX's collectives and lax.ppermute only.
A program may use at most 64 MiB of HBM per device.

```python
import jax
import jax.numpy as jnp
import numpy as np
from jax import lax

P_DEV = 128
RHS = 512
RANK = 256
ROW_LEVELS = 2
COL_LEVELS = 3
LEVELS = 5
GROUPS = 512
POINTS = 65536
N_ROW = 16
N_COL = 32


def draw_residual_in(key, part):
    folded = jax.random.fold_in(key, 17)
    key_rotation = jax.random.fold_in(folded, 1)
    key_bulk = jax.random.fold_in(folded, 2)
    rotation = jnp.linalg.qr(jax.random.normal(key_rotation, (RHS, RHS), jnp.float32))[0]
    spread_vals = 10.0 ** jnp.linspace(0.0, -2.0, RHS, dtype=jnp.float32)
    spread_vals = spread_vals / jnp.sqrt(jnp.mean(spread_vals * spread_vals))
    mixing = jnp.dot(rotation * spread_vals[None, :], rotation.T, precision=lax.Precision.HIGHEST)
    bulk_draw = jax.random.normal(key_bulk, (POINTS, RHS), jnp.float32)
    col_scales = jnp.ones((RHS,), jnp.float32)
    mixed = jnp.dot(bulk_draw, mixing, precision=lax.Precision.HIGHEST) * col_scales[None, :]
    return jnp.clip(mixed, -6.0, 6.0)


def touch_ends(array, stream_key, smallest, largest):
    longest = array.shape.index(max(array.shape))
    spots = []
    for shift in (0, 1):
        where = [jax.random.randint(jax.random.fold_in(stream_key, axis), (), 0, length) for axis, length in enumerate(array.shape)]
        where[longest] = (where[longest] + shift) % array.shape[longest]
        spots.append(tuple(where))
    return array.at[spots[0]].set(smallest).at[spots[1]].set(largest)


def block_scale(key, dims, split, low, top_value):
    factor_of = 1.0
    for dim, blocks in split:
        heights = jax.random.uniform(jax.random.fold_in(jax.random.fold_in(key, 6), dim), (blocks,), jnp.float32, low / len(split), top_value / len(split))
        factor_of = factor_of * jnp.repeat(jnp.exp(heights), dims[dim] // blocks).reshape((-1,) + (1,) * (len(dims) - 1 - dim))
    return factor_of


def centred(rng, dims, width, reach, pieces=(), kind=jnp.bfloat16):
    gain = block_scale(rng, dims, pieces, -0.22, 0.18) if pieces else 1.0
    drawn = jax.random.normal(rng, dims, jnp.float32) * width * gain
    return jnp.minimum(jnp.maximum(drawn, -reach), reach).astype(kind)


def setup_inputs(seed: int = 0) -> dict:
    splits = jax.random.split(jax.random.key(seed), 9)
    coords = jnp.clip(jax.random.uniform(splits[0], (3, POINTS), jnp.float32, -1.0, 1.0) * block_scale(splits[0], (3, POINTS), ((1, 512),), -0.4, 0.0), -1.0, 1.0)
    residual_in = draw_residual_in(jax.random.fold_in(splits[8], 71), 0)
    link_mask = touch_ends((jax.random.randint(splits[2], (GROUPS, 2), 0, 4) < 3).astype(jnp.int32), jax.random.fold_in(splits[2], 1), 0, 1)
    compress = centred(splits[3], (POINTS, RANK), P_DEV ** -0.5, 0.5, ((0, 512),), jnp.float32)
    expand = centred(splits[4], (POINTS, RANK), RANK ** -0.5, 0.375, ((0, 512),), jnp.float32)
    level_gain = jnp.clip(1.0 + 0.1 * jax.random.normal(splits[5], (GROUPS, LEVELS * RANK), jnp.float32), 0.5, 1.5)
    level_couple = centred(splits[6], (GROUPS * RANK, LEVELS * RANK), (4 * RANK) ** -0.5, 0.1875, ((0, 512),), jnp.float32)
    partner_perm = jax.vmap(lambda own: jax.random.permutation(own, RANK))(jax.random.split(splits[7], GROUPS * LEVELS)).reshape((GROUPS, LEVELS, RANK)).astype(jnp.int32)
    return {"coords": coords, "residual_in": residual_in, "link_mask": link_mask, "compress": compress, "expand": expand, "level_gain": level_gain, "level_couple": level_couple, "partner_perm": partner_perm}


WAVENUM = 6.0
SOFTEN = 0.01

def kernel_tile(own_xyz, other_xyz):
    dist_sq = (own_xyz[0][:, None] - other_xyz[0][None, :]) ** 2
    dist_sq = dist_sq + (own_xyz[1][:, None] - other_xyz[1][None, :]) ** 2
    dist_sq = dist_sq + (own_xyz[2][:, None] - other_xyz[2][None, :]) ** 2
    return jnp.cos(WAVENUM * jnp.sqrt(dist_sq)) / jnp.sqrt(dist_sq + SOFTEN)

def matmul_hi(left, right):
    return jnp.dot(left, right, precision=lax.Precision.HIGHEST)

def chol_solve(gram_mat, cross_mat):
    factor = jnp.linalg.cholesky(gram_mat)
    middle = lax.linalg.triangular_solve(factor, cross_mat, left_side=True, lower=True)
    return lax.linalg.triangular_solve(factor, middle, left_side=True, lower=True, transpose_a=True)

def reference(coords, residual_in, link_mask, compress, expand, level_gain, level_couple, partner_perm):
    groups_all = N_ROW * N_COL
    blocks = residual_in.reshape(groups_all, P_DEV, RHS)
    xyz = coords.reshape(3, groups_all, P_DEV).transpose(1, 0, 2)
    zero_rhs = jnp.zeros((1, P_DEV, RHS), blocks.dtype)
    zero_xyz = jnp.zeros((1, 3, P_DEV), xyz.dtype)
    below_rhs = jnp.concatenate([zero_rhs, blocks[:-1]], axis=0)
    above_rhs = jnp.concatenate([blocks[1:], zero_rhs], axis=0)
    below_xyz = jnp.concatenate([zero_xyz, xyz[:-1]], axis=0)
    above_xyz = jnp.concatenate([xyz[1:], zero_xyz], axis=0)
    weights = link_mask.astype(blocks.dtype)
    near_scale = (3.0 * P_DEV) ** (-0.5)

    def near_one(items):
        own_xyz, low_xyz, high_xyz, own_rhs, low_rhs, high_rhs, mask_row = items
        total = matmul_hi(kernel_tile(own_xyz, own_xyz), own_rhs)
        total = total + mask_row[0] * matmul_hi(kernel_tile(own_xyz, low_xyz), low_rhs)
        total = total + mask_row[1] * matmul_hi(kernel_tile(own_xyz, high_xyz), high_rhs)
        return near_scale * total
    near_field = lax.map(near_one, (xyz, below_xyz, above_xyz, blocks, below_rhs, above_rhs, weights))
    comp_blocks = compress.reshape(groups_all, P_DEV, RANK)
    exp_blocks = expand.reshape(groups_all, P_DEV, RANK)
    couple_blocks = level_couple.reshape(groups_all, RANK, LEVELS * RANK)
    coeffs = jnp.einsum('dpk,dpr->dkr', comp_blocks, blocks, precision=lax.Precision.HIGHEST)
    group_ids = np.arange(groups_all)
    col_bits = N_COL.bit_length() - 1
    flips = []
    for index_row in range(ROW_LEVELS):
        flips.append(1 << N_ROW.bit_length() - 2 - index_row + col_bits)
    for index_col in range(COL_LEVELS):
        flips.append(1 << N_COL.bit_length() - 2 - index_col)
    for level_at in range(LEVELS):
        partner = coeffs[group_ids ^ flips[level_at]]
        picked = jnp.take_along_axis(partner, partner_perm[:, level_at, :, None].astype(jnp.int32), axis=1)
        gain_col = level_gain[:, level_at * RANK:(level_at + 1) * RANK][:, :, None]
        couple = couple_blocks[:, :, level_at * RANK:(level_at + 1) * RANK]
        coeffs = gain_col * coeffs + jnp.einsum('dkj,djr->dkr', couple, picked, precision=lax.Precision.HIGHEST)
    far_field = jnp.einsum('dpk,dkr->dpr', exp_blocks, coeffs, precision=lax.Precision.HIGHEST)
    image = (2.0 * blocks + near_field + far_field).reshape(POINTS, RHS)
    gram_mat = matmul_hi(image.T, image)
    cross_mat = matmul_hi(image.T, residual_in)
    alpha_mix = chol_solve(gram_mat, cross_mat)
    new_residual = residual_in - matmul_hi(image, alpha_mix)
    res_norms = jnp.sqrt(lax.optimization_barrier(jnp.sum(new_residual * new_residual, axis=0)) / POINTS)
    return (new_residual, res_norms)
```

```python
import functools

import jax
import jax.numpy as jnp
from jax import lax
from jax.experimental import pallas as pl
from jax.experimental.pallas import tpu as pltpu
from jax.sharding import PartitionSpec as P

ROW_LEVELS = 2
COL_LEVELS = 3


WAVENUM = 6.0
SOFTEN = 0.01
PIVOT = 128
SLAB = 8


def in_blocks(shard, dim, length):
    shape = shard.shape
    tiles = shard.reshape(*shape[:dim], length, shape[dim] // length, *shape[dim + 1 :])
    return jnp.moveaxis(tiles, dim, 0)


def sent_and_summed(shard, axis, dim):
    length = lax.axis_size(axis)
    tiles = lax.all_to_all(in_blocks(shard, dim, length), axis, 0, 0, tiled=True)
    return jnp.sum(tiles, axis=0)


def side_by_side(arrays, axis, dim, along):
    widths = [a.shape[along] for a in arrays]
    both = jnp.concatenate(arrays, axis=along)
    whole = sent_and_summed(both, axis, dim)
    return tuple(jnp.split(whole, [sum(widths[:k]) for k in range(1, len(widths))], axis=along))


def from_everyone(shard, axis):
    length = lax.axis_size(axis)
    return lax.all_to_all(
        jnp.broadcast_to(shard[None], (length, *shard.shape)), axis, 0, 0, tiled=True
    )


def over_copies(shard, axis):
    return from_everyone(shard, axis).sum(axis=0)


def packed_total(arrays, axis):
    ends = [0]
    for a in arrays:
        ends.append(ends[-1] + a.size)
    so_far = over_copies(jnp.concatenate([a.ravel() for a in arrays]), axis)
    return tuple((so_far[b:e].reshape(a.shape) for a, b, e in zip(arrays, ends, ends[1:])))


def gather_turned(arrays, axis, dims):
    turned = [jnp.moveaxis(a, dim, 0) for a, dim in zip(arrays, dims)]
    both = jnp.concatenate([t.reshape(len(t), -1) for t in turned], axis=1)
    whole, at, finished = (lax.all_gather(both, axis, axis=0, tiled=True), 0, [])
    for t, dim in zip(turned, dims):
        piece = whole[:, at : at + t[0].size].reshape(-1, *t.shape[1:])
        finished.append(jnp.moveaxis(piece, 0, dim))
        at += t[0].size
    return tuple(finished)


def from_behind(block, axis, distance):
    devices = range(lax.axis_size(axis))
    route = [(i - distance, i) for i in devices if i - distance in devices]
    return lax.ppermute(block, axis, route)


def from_partner(block, axis, distance):
    count = lax.axis_size(axis)
    route = []
    for low in range(count):
        high = low | 1 << distance
        if high != low and high < count:
            route += [(low, high), (high, low)]
    return lax.ppermute(block, axis, route)


def kernel_tile(own_xyz, other_xyz):
    dist_sq = (own_xyz[0][:, None] - other_xyz[0][None, :]) ** 2
    dist_sq = dist_sq + (own_xyz[1][:, None] - other_xyz[1][None, :]) ** 2
    dist_sq = dist_sq + (own_xyz[2][:, None] - other_xyz[2][None, :]) ** 2
    return jnp.cos(WAVENUM * jnp.sqrt(dist_sq)) / jnp.sqrt(dist_sq + SOFTEN)


def matmul_hi(left, right):
    return jnp.dot(left, right, precision=lax.Precision.HIGHEST)


def inner_cols(left, right):
    return lax.dot_general(left, right, (((0,), (0,)), ((), ())), precision=lax.Precision.HIGHEST)


def dot_f32(left, right, left_dim, right_dim):
    return lax.dot_general(
        left,
        right,
        (((left_dim,), (right_dim,)), ((), ())),
        precision=lax.Precision.HIGHEST,
        preferred_element_type=jnp.float32,
    )


def three_parts(value):
    high = value.astype(jnp.bfloat16).astype(jnp.float32)
    middle = (value - high).astype(jnp.bfloat16).astype(jnp.float32)
    return high, middle, (value - high) - middle


def self_product(rows, first, count):
    high, middle, low = three_parts(rows)
    right = jnp.concatenate([high, middle, high, low, high, middle], axis=0)
    left = jnp.concatenate([high, high, middle, high, low, middle], axis=0)[:, first:count]
    return lax.dot_general(
        left.astype(jnp.bfloat16),
        right.astype(jnp.bfloat16),
        (((0,), (0,)), ((), ())),
        preferred_element_type=jnp.float32,
    )


def slab_factor_inverse(slab, at):
    spread = (8, 128)
    block, beside, found = {}, {}, {}
    for i in range(SLAB):
        beside[i, i] = jnp.ones(spread, jnp.float32)
        for j in range(i, SLAB):
            block[i, j] = jnp.broadcast_to(slab[i : i + 1, at + j : at + j + 1], spread)
    for k in range(SLAB):
        pivot = 1.0 / block[k, k]
        for i in range(k + 1, SLAB):
            ratio = block[k, i] * pivot
            for j in range(i, SLAB):
                block[i, j] = block[i, j] - ratio * block[k, j]
            for j in range(k + 1):
                term = ratio * beside[k, j] if j < k else ratio
                beside[i, j] = beside[i, j] - term if (i, j) in beside else -term
    for i in range(SLAB):
        scale = lax.rsqrt(block[i, i])
        for j in range(i + 1):
            found[i, j] = beside[i, j] * scale if j < i else scale
    return found


def slab_rows(found, slab, count):
    row_at = lax.broadcasted_iota(jnp.int32, (SLAB, count), 0)
    left, right = 0.0, 0.0
    for j in range(SLAB):
        column = jnp.zeros((SLAB, count), jnp.float32)
        for i in range(j, SLAB):
            column = jnp.where(row_at == i, found[i, j], column)
        left = left + column * jnp.broadcast_to(slab[j : j + 1, :count], (SLAB, count))
        right = right + column * jnp.broadcast_to(slab[j : j + 1, count:], (SLAB, count))
    return jnp.concatenate([left, right], axis=1)


def factor_inverse(block):
    count = block.shape[0]
    row_at = lax.broadcasted_iota(jnp.int32, block.shape, 0)
    col_at = lax.broadcasted_iota(jnp.int32, block.shape, 1)
    rest = jnp.concatenate([block, jnp.where(row_at == col_at, 1.0, 0.0)], axis=1)
    done = []
    for at in range(0, count, SLAB):
        slab = rest[:SLAB]
        rows = slab_rows(slab_factor_inverse(slab, at), slab, count)
        done.append(rows[:, count:])
        if at + SLAB < count:
            rest = rest[SLAB:] - self_product(rows, at + SLAB, count)
    return jnp.concatenate(done, axis=0)


def eliminate(points_total, gram_in, cross_in, image_in, own_in, total_in, new, norms, gram, cross, image):
    gram[...] = gram_in[...]
    cross[...] = cross_in[...]
    image[...] = image_in[...]
    new[...] = own_in[...]
    left_over = total_in[...]
    size = gram.shape[0]
    for at in range(0, size, PIVOT):
        end = at + PIVOT
        inverse = factor_inverse(gram[at:end, at:end])
        cross_rows = dot_f32(inverse, cross[at:end, :], 1, 0)
        image_cols = dot_f32(image[:, at:end], inverse, 1, 1)
        left_over = left_over - jnp.sum(cross_rows * cross_rows, axis=0, keepdims=True)
        new[...] -= dot_f32(image_cols, cross_rows, 1, 0)
        if end < size:
            gram_rows = dot_f32(inverse, gram[at:end, end:], 1, 0)
            image[:, end:] -= dot_f32(image_cols, gram_rows, 1, 0)
            cross[end:, :] -= dot_f32(gram_rows, cross_rows, 0, 0)
            for row in range(end, size, PIVOT):
                part = gram_rows[:, row - end : row - end + PIVOT]
                gram[row : row + PIVOT, row:] -= dot_f32(part, gram_rows[:, row - end :], 0, 0)
    norms[...] = jnp.sqrt(left_over / points_total)


def project_out(gram_mat, cross_mat, image, own, total, points_total):
    return pl.pallas_call(
        functools.partial(eliminate, points_total),
        out_shape=(
            jax.ShapeDtypeStruct(own.shape, jnp.float32),
            jax.ShapeDtypeStruct(total.shape, jnp.float32),
        ),
        scratch_shapes=[
            pltpu.VMEM(gram_mat.shape, jnp.float32),
            pltpu.VMEM(cross_mat.shape, jnp.float32),
            pltpu.VMEM(image.shape, jnp.float32),
        ],
        compiler_params=pltpu.CompilerParams(vmem_limit_bytes=40 * 2**20),
        name="eliminate",
    )(gram_mat, cross_mat, image, own, total)


def global_sum(members):
    shares = side_by_side((members[0], members[1], members[2]), "col", 1, 0)
    shares = packed_total((shares[0], shares[1], shares[2]), "row")
    return gather_turned((shares[0], shares[1], shares[2]), "col", (1, 1, 1))


def shards(
    coords, residual_in, link_mask, compress, expand, level_gain, level_couple, partner_perm
):
    below_xyz, below_rhs = from_behind((coords, residual_in), ("row", "col"), 1)
    above_xyz, above_rhs = from_behind((coords, residual_in), ("row", "col"), -1)
    rank_width = compress.shape[1]
    coeffs = inner_cols(compress, residual_in)

    def mix_level(current, partner, level_at):
        taken_rows = partner_perm[0, level_at]
        picked = jnp.take(partner, taken_rows, axis=0)
        gain_col = level_gain[0, level_at * rank_width : (level_at + 1) * rank_width][:, None]
        couple = level_couple[:, level_at * rank_width : (level_at + 1) * rank_width]
        return gain_col * current + matmul_hi(couple, picked)

    row_top = lax.axis_size("row").bit_length() - 2
    for index_row in range(ROW_LEVELS):
        partner = from_partner(coeffs, "row", row_top - index_row)
        coeffs = mix_level(coeffs, partner, index_row)
    col_top = lax.axis_size("col").bit_length() - 2
    for index_col in range(COL_LEVELS):
        partner = from_partner(coeffs, "col", col_top - index_col)
        coeffs = mix_level(coeffs, partner, ROW_LEVELS + index_col)
    far_field = matmul_hi(expand, coeffs)
    weights = link_mask.astype(jnp.float32)
    near_scale = (3.0 * coords.shape[1]) ** (-0.5)
    near_field = matmul_hi(kernel_tile(coords, coords), residual_in)
    near_field = near_field + weights[0, 0] * matmul_hi(kernel_tile(coords, below_xyz), below_rhs)
    near_field = near_field + weights[0, 1] * matmul_hi(kernel_tile(coords, above_xyz), above_rhs)
    near_field = near_scale * near_field
    image = 2.0 * residual_in + near_field + far_field
    gram_mat = inner_cols(image, image)
    cross_mat = inner_cols(image, residual_in)
    points_total = coords.shape[1] * lax.axis_size("row") * lax.axis_size("col")
    self_squares = jnp.sum(residual_in * residual_in, axis=0)[None, :]
    gram_mat, cross_mat, self_total = global_sum((gram_mat, cross_mat, self_squares))
    new_residual, res_norms = project_out(
        gram_mat, cross_mat, image, residual_in, self_total, points_total
    )
    return (new_residual, res_norms[0])


def solution(mesh):
    return jax.shard_map(
        shards,
        mesh=mesh,
        in_specs=(
            P(None, ("row", "col")),
            P(("row", "col"), None),
            P(("row", "col"), None),
            P(("row", "col"), None),
            P(("row", "col"), None),
            P(("row", "col"), None),
            P(("row", "col"), None),
            P(("row", "col"), None, None),
        ),
        out_specs=(P(("row", "col"), None), P()),
        check_vma=False,
    )
```

```python
import functools

import jax
import jax.numpy as jnp
from jax import lax
from jax.experimental import pallas as pl
from jax.experimental.pallas import tpu as pltpu
from jax.sharding import PartitionSpec as P

LEVELS = 5
CHUNKS = 2


WAVENUM = 6.0
SOFTEN = 0.01
PIVOT = 128
SLAB = 8


def swapped(block, axis, bits):
    return lax.ppermute(block, axis, [(i, i ^ bits) for i in range(lax.axis_size(axis))])


def from_behind(block, axis, distance):
    devices = range(lax.axis_size(axis))
    route = [(i - distance, i) for i in devices if i - distance in devices]
    return lax.ppermute(block, axis, route)


def kernel_tile(own_xyz, other_xyz):
    dist_sq = (own_xyz[0][:, None] - other_xyz[0][None, :]) ** 2
    dist_sq = dist_sq + (own_xyz[1][:, None] - other_xyz[1][None, :]) ** 2
    dist_sq = dist_sq + (own_xyz[2][:, None] - other_xyz[2][None, :]) ** 2
    return jnp.cos(WAVENUM * jnp.sqrt(dist_sq)) / jnp.sqrt(dist_sq + SOFTEN)


def matmul_hi(left, right, left_dim=1, right_dim=0):
    dims = (((left_dim,), (right_dim,)), ((), ()))
    return lax.dot_general(left, right, dims, precision=lax.Precision.HIGHEST)


def dot_f32(left, right, left_dim, right_dim):
    return lax.dot_general(
        left,
        right,
        (((left_dim,), (right_dim,)), ((), ())),
        precision=lax.Precision.HIGHEST,
        preferred_element_type=jnp.float32,
    )


def three_parts(value):
    high = value.astype(jnp.bfloat16).astype(jnp.float32)
    middle = (value - high).astype(jnp.bfloat16).astype(jnp.float32)
    return high, middle, (value - high) - middle


def self_product(rows, first, count):
    high, middle, low = three_parts(rows)
    right = jnp.concatenate([high, middle, high, low, high, middle], axis=0)
    left = jnp.concatenate([high, high, middle, high, low, middle], axis=0)[:, first:count]
    return lax.dot_general(
        left.astype(jnp.bfloat16),
        right.astype(jnp.bfloat16),
        (((0,), (0,)), ((), ())),
        preferred_element_type=jnp.float32,
    )


def slab_factor_inverse(slab, at):
    spread = (8, 128)
    block, beside, found = {}, {}, {}
    for i in range(SLAB):
        beside[i, i] = jnp.ones(spread, jnp.float32)
        for j in range(i, SLAB):
            block[i, j] = jnp.broadcast_to(slab[i : i + 1, at + j : at + j + 1], spread)
    for k in range(SLAB):
        pivot = 1.0 / block[k, k]
        for i in range(k + 1, SLAB):
            ratio = block[k, i] * pivot
            for j in range(i, SLAB):
                block[i, j] = block[i, j] - ratio * block[k, j]
            for j in range(k + 1):
                term = ratio * beside[k, j] if j < k else ratio
                beside[i, j] = beside[i, j] - term if (i, j) in beside else -term
    for i in range(SLAB):
        scale = lax.rsqrt(block[i, i])
        for j in range(i + 1):
            found[i, j] = beside[i, j] * scale if j < i else scale
    return found


def slab_rows(found, slab, count):
    row_at = lax.broadcasted_iota(jnp.int32, (SLAB, count), 0)
    left, right = 0.0, 0.0
    for j in range(SLAB):
        column = jnp.zeros((SLAB, count), jnp.float32)
        for i in range(j, SLAB):
            column = jnp.where(row_at == i, found[i, j], column)
        left = left + column * jnp.broadcast_to(slab[j : j + 1, :count], (SLAB, count))
        right = right + column * jnp.broadcast_to(slab[j : j + 1, count:], (SLAB, count))
    return jnp.concatenate([left, right], axis=1)


def factor_inverse(block):
    count = block.shape[0]
    row_at = lax.broadcasted_iota(jnp.int32, block.shape, 0)
    col_at = lax.broadcasted_iota(jnp.int32, block.shape, 1)
    rest = jnp.concatenate([block, jnp.where(row_at == col_at, 1.0, 0.0)], axis=1)
    done = []
    for at in range(0, count, SLAB):
        slab = rest[:SLAB]
        rows = slab_rows(slab_factor_inverse(slab, at), slab, count)
        done.append(rows[:, count:])
        if at + SLAB < count:
            rest = rest[SLAB:] - self_product(rows, at + SLAB, count)
    return jnp.concatenate(done, axis=0)


def eliminate(
    points_total, core, mine, theirs, image_in, own_in, new, norms, gram, cross, image, total
):
    size = gram.shape[0]
    image[...] = image_in[...]
    new[...] = own_in[...]

    def unpack(first, second):
        gram[0:128, 0:512] = first[:, 0:512]
        gram[384:512, 384:512] = first[:, 512:640]
        gram[128:256, 128:512] = second[:, 0:384]
        gram[256:384, 256:512] = second[:, 384:640]
        cross[0:128, :] = first[:, 640:1152]
        cross[128:256, :] = first[:, 1152:1664]
        cross[256:384, :] = second[:, 640:1152]
        cross[384:512, :] = second[:, 1152:1664]
        for piece in range(4):
            total[:, piece * 128 : piece * 128 + 128] = first[piece : piece + 1, 1664:1792]

    @pl.when(core[0] == 0)
    def _():
        unpack(mine, theirs)

    @pl.when(core[0] == 1)
    def _():
        unpack(theirs, mine)

    left_over = total[...]
    for at in range(0, size, PIVOT):
        end = at + PIVOT
        inverse = factor_inverse(gram[at:end, at:end])
        cross_rows = dot_f32(inverse, cross[at:end, :], 1, 0)
        image_cols = dot_f32(image[:, at:end], inverse, 1, 1)
        left_over = left_over - jnp.sum(cross_rows * cross_rows, axis=0, keepdims=True)
        new[...] -= dot_f32(image_cols, cross_rows, 1, 0)
        if end < size:
            gram_rows = dot_f32(inverse, gram[at:end, end:], 1, 0)
            image[:, end:] -= dot_f32(image_cols, gram_rows, 1, 0)
            cross[end:, :] -= dot_f32(gram_rows, cross_rows, 0, 0)
            for row in range(end, size, PIVOT):
                part = gram_rows[:, row - end : row - end + PIVOT]
                gram[row : row + PIVOT, row:] -= dot_f32(part, gram_rows[:, row - end :], 0, 0)
    norms[...] = jnp.sqrt(left_over / points_total)


def project_out(core, mine, theirs, image, own, points_total):
    size = own.shape[1]
    whole = pl.BlockSpec(memory_space=pltpu.VMEM)
    return pl.pallas_call(
        functools.partial(eliminate, points_total),
        in_specs=[pl.BlockSpec(memory_space=pltpu.SMEM), whole, whole, whole, whole],
        out_specs=(whole, whole),
        out_shape=(
            jax.ShapeDtypeStruct(own.shape, jnp.float32),
            jax.ShapeDtypeStruct((1, size), jnp.float32),
        ),
        scratch_shapes=[
            pltpu.VMEM((size, size), jnp.float32),
            pltpu.VMEM((size, size), jnp.float32),
            pltpu.VMEM(image.shape, jnp.float32),
            pltpu.VMEM((1, size), jnp.float32),
        ],
        compiler_params=pltpu.CompilerParams(vmem_limit_bytes=40 * 2**20),
        name="eliminate",
    )(core[None], mine, theirs, image, own)


def plane_groups():
    return [[2 * chip + core for chip in range(lax.axis_size("col") // 2)] for core in range(2)]


def within_plane(tiles):
    return lax.all_to_all(tiles, "col", 0, 0, axis_index_groups=plane_groups(), tiled=True)


def quad_sum(share, unit):
    one, two, three = (swapped(share, "row", unit * k) for k in (1, 2, 3))
    return (share + one) + (two + three)


def global_sum(half):
    chips = lax.axis_size("col") // 2
    rows = half.shape[0] // chips
    share = jnp.sum(within_plane(half.reshape(chips, rows, -1)), axis=0)
    share = quad_sum(quad_sum(share, 1), 4)
    return within_plane(jnp.broadcast_to(share[None], (chips, *share.shape))).reshape(half.shape)


def half_of_sums(core, image, own, pair_image, pair_own, own_squares):
    odd = core == 1
    images = jnp.concatenate([image, pair_image], axis=0)
    owns = jnp.concatenate([own, pair_own], axis=0)
    blocks = [images[:, k * 128 : k * 128 + 128] for k in range(4)]
    wide = matmul_hi(jnp.where(odd, blocks[1], blocks[0]), images, 0, 0)
    narrow = matmul_hi(jnp.where(odd, blocks[2], blocks[3]), images[:, 256:], 0, 0)
    gram_part = jnp.where(
        odd,
        jnp.concatenate([wide[:, 128:], narrow], axis=1),
        jnp.concatenate([wide, narrow[:, 128:]], axis=1),
    )
    cross_part = matmul_hi(jnp.where(odd, images[:, 256:], images[:, :256]), owns, 0, 0)
    squares = jnp.pad(own_squares.reshape(4, 128), ((0, 124), (0, 0)))
    return jnp.concatenate([gram_part, cross_part[:128], cross_part[128:], squares], axis=1)


def shards(
    coords, residual_in, link_mask, compress, expand, level_gain, level_couple, partner_perm
):
    rank = compress.shape[1]
    chunks = jnp.split(residual_in, CHUNKS, axis=1)
    core = lax.axis_index("col") & 1

    by_three = [swapped(chunk, "row", 12) for chunk in chunks]
    compress_two = swapped(compress, "row", 8)
    by_two = [swapped(chunk, "row", 4) for chunk in by_three]
    by_one = [swapped(chunk, "row", 12) for chunk in by_two]

    below_xyz, below_rhs = from_behind((coords, residual_in), ("row", "col"), 1)
    above_xyz, above_rhs = from_behind((coords, residual_in), ("row", "col"), -1)

    gains = [level_gain[0, k * rank : (k + 1) * rank][:, None] for k in range(LEVELS)]
    numbers = jnp.arange(rank, dtype=jnp.int32)[None, :]

    def couple_of(level_at):
        couple = level_couple[:, level_at * rank : (level_at + 1) * rank]
        place = (partner_perm[0, level_at][:, None] == numbers).astype(jnp.float32)
        return matmul_hi(couple, place)

    couples = [couple_of(k) for k in range(LEVELS)]
    last_partner = swapped(matmul_hi(expand, couples[4]), "col", 4)
    last_own = expand * level_gain[:, 4 * rank :]

    low_map = jnp.concatenate(
        [gains[0] * compress.T, matmul_hi(couples[0], compress_two, 1, 1)], axis=1
    )
    low_map_one = matmul_hi(couples[1], swapped(low_map, "row", 4))
    low_map_own = gains[1] * low_map

    near_scale = (3.0 * coords.shape[1]) ** (-0.5)
    weights = link_mask.astype(jnp.float32)
    near_field = matmul_hi(kernel_tile(coords, coords), residual_in)
    near_field = near_field + weights[0, 0] * matmul_hi(kernel_tile(coords, below_xyz), below_rhs)
    near_field = near_field + weights[0, 1] * matmul_hi(kernel_tile(coords, above_xyz), above_rhs)
    base = 2.0 * residual_in + near_scale * near_field
    own_squares = jnp.sum(residual_in * residual_in, axis=0)
    pair_own = jnp.where(core == 1, below_rhs, above_rhs)
    pair_squares = jnp.sum(pair_own * pair_own, axis=0)

    far_parts = []
    for own, one, two, three in zip(chunks, by_one, by_two, by_three):
        coeffs = matmul_hi(low_map_own, jnp.concatenate([own, two], axis=0))
        coeffs = coeffs + matmul_hi(low_map_one, jnp.concatenate([one, three], axis=0))
        coeffs = gains[2] * coeffs + matmul_hi(couples[2], swapped(coeffs, "col", 16))
        coeffs = gains[3] * coeffs + matmul_hi(couples[3], swapped(coeffs, "col", 8))
        sent = swapped(matmul_hi(last_partner, coeffs), "col", 4)
        far_parts.append(matmul_hi(last_own, coeffs) + sent)
    image = base + jnp.concatenate(far_parts, axis=1)

    half = half_of_sums(
        core, image, residual_in, swapped(image, "col", 1), pair_own, own_squares + pair_squares
    )
    mine = global_sum(half)
    theirs = swapped(mine, "col", 1)
    points_total = coords.shape[1] * lax.axis_size("row") * lax.axis_size("col")
    new_residual, res_norms = project_out(core, mine, theirs, image, residual_in, points_total)
    return (new_residual, res_norms[0])


def solution(mesh):
    return jax.shard_map(
        shards,
        mesh=mesh,
        in_specs=(
            P(None, ("row", "col")),
            P(("row", "col"), None),
            P(("row", "col"), None),
            P(("row", "col"), None),
            P(("row", "col"), None),
            P(("row", "col"), None),
            P(("row", "col"), None),
            P(("row", "col"), None, None),
        ),
        out_specs=(P(("row", "col"), None), P()),
        check_vma=False,
    )
```

```python
import functools

import jax
import jax.numpy as jnp
from jax import lax
from jax.experimental import pallas as pl
from jax.experimental.pallas import tpu as pltpu
from jax.sharding import PartitionSpec as P

LEVELS = 5


WAVENUM = 6.0
SOFTEN = 0.01
PIVOT = 128
SLAB = 8


def swapped(block, axis, bits):
    return lax.ppermute(block, axis, [(i, i ^ bits) for i in range(lax.axis_size(axis))])


def from_behind(block, axis, distance):
    devices = range(lax.axis_size(axis))
    route = [(i - distance, i) for i in devices if i - distance in devices]
    return lax.ppermute(block, axis, route)


def kernel_tile(own_xyz, other_xyz):
    dist_sq = (own_xyz[0][:, None] - other_xyz[0][None, :]) ** 2
    dist_sq = dist_sq + (own_xyz[1][:, None] - other_xyz[1][None, :]) ** 2
    dist_sq = dist_sq + (own_xyz[2][:, None] - other_xyz[2][None, :]) ** 2
    return jnp.cos(WAVENUM * jnp.sqrt(dist_sq)) / jnp.sqrt(dist_sq + SOFTEN)


def matmul_hi(left, right, left_dim=1, right_dim=0):
    dims = (((left_dim,), (right_dim,)), ((), ()))
    return lax.dot_general(left, right, dims, precision=lax.Precision.HIGHEST)


def dot_f32(left, right, left_dim, right_dim):
    return lax.dot_general(
        left,
        right,
        (((left_dim,), (right_dim,)), ((), ())),
        precision=lax.Precision.HIGHEST,
        preferred_element_type=jnp.float32,
    )


def three_parts(value):
    high = value.astype(jnp.bfloat16).astype(jnp.float32)
    middle = (value - high).astype(jnp.bfloat16).astype(jnp.float32)
    return high, middle, (value - high) - middle


def self_product(rows, first, count):
    high, middle, low = three_parts(rows)
    right = jnp.concatenate([high, middle, high, low, high, middle], axis=0)
    left = jnp.concatenate([high, high, middle, high, low, middle], axis=0)[:, first:count]
    return lax.dot_general(
        left.astype(jnp.bfloat16),
        right.astype(jnp.bfloat16),
        (((0,), (0,)), ((), ())),
        preferred_element_type=jnp.float32,
    )


def slab_factor_inverse(slab, at):
    spread = (8, 128)
    block, beside, found = {}, {}, {}
    for i in range(SLAB):
        beside[i, i] = jnp.ones(spread, jnp.float32)
        for j in range(i, SLAB):
            block[i, j] = jnp.broadcast_to(slab[i : i + 1, at + j : at + j + 1], spread)
    for k in range(SLAB):
        pivot = 1.0 / block[k, k]
        for i in range(k + 1, SLAB):
            ratio = block[k, i] * pivot
            for j in range(i, SLAB):
                block[i, j] = block[i, j] - ratio * block[k, j]
            for j in range(k + 1):
                term = ratio * beside[k, j] if j < k else ratio
                beside[i, j] = beside[i, j] - term if (i, j) in beside else -term
    for i in range(SLAB):
        scale = lax.rsqrt(block[i, i])
        for j in range(i + 1):
            found[i, j] = beside[i, j] * scale if j < i else scale
    return found


def slab_rows(found, slab, count):
    row_at = lax.broadcasted_iota(jnp.int32, (SLAB, count), 0)
    left, right = 0.0, 0.0
    for j in range(SLAB):
        column = jnp.zeros((SLAB, count), jnp.float32)
        for i in range(j, SLAB):
            column = jnp.where(row_at == i, found[i, j], column)
        left = left + column * jnp.broadcast_to(slab[j : j + 1, :count], (SLAB, count))
        right = right + column * jnp.broadcast_to(slab[j : j + 1, count:], (SLAB, count))
    return jnp.concatenate([left, right], axis=1)


def factor_inverse(block):
    count = block.shape[0]
    row_at = lax.broadcasted_iota(jnp.int32, block.shape, 0)
    col_at = lax.broadcasted_iota(jnp.int32, block.shape, 1)
    rest = jnp.concatenate([block, jnp.where(row_at == col_at, 1.0, 0.0)], axis=1)
    done = []
    for at in range(0, count, SLAB):
        slab = rest[:SLAB]
        rows = slab_rows(slab_factor_inverse(slab, at), slab, count)
        done.append(rows[:, count:])
        if at + SLAB < count:
            rest = rest[SLAB:] - self_product(rows, at + SLAB, count)
    return jnp.concatenate(done, axis=0)


def eliminate(
    points_total, core, mine, theirs, image_in, own_in, new, norms, gram, cross, image, total
):
    size = gram.shape[0]
    image[...] = image_in[...]
    new[...] = own_in[...]

    def unpack(first, second):
        gram[0:128, 0:512] = first[:, 0:512]
        gram[384:512, 384:512] = first[:, 512:640]
        gram[128:256, 128:512] = second[:, 0:384]
        gram[256:384, 256:512] = second[:, 384:640]
        cross[0:128, :] = first[:, 640:1152]
        cross[128:256, :] = first[:, 1152:1664]
        cross[256:384, :] = second[:, 640:1152]
        cross[384:512, :] = second[:, 1152:1664]
        for piece in range(4):
            total[:, piece * 128 : piece * 128 + 128] = first[piece : piece + 1, 1664:1792]

    @pl.when(core[0] == 0)
    def _():
        unpack(mine, theirs)

    @pl.when(core[0] == 1)
    def _():
        unpack(theirs, mine)

    left_over = total[...]
    for at in range(0, size, PIVOT):
        end = at + PIVOT
        inverse = factor_inverse(gram[at:end, at:end])
        cross_rows = dot_f32(inverse, cross[at:end, :], 1, 0)
        image_cols = dot_f32(image[:, at:end], inverse, 1, 1)
        left_over = left_over - jnp.sum(cross_rows * cross_rows, axis=0, keepdims=True)
        new[...] -= dot_f32(image_cols, cross_rows, 1, 0)
        if end < size:
            gram_rows = dot_f32(inverse, gram[at:end, end:], 1, 0)
            image[:, end:] -= dot_f32(image_cols, gram_rows, 1, 0)
            cross[end:, :] -= dot_f32(gram_rows, cross_rows, 0, 0)
            for row in range(end, size, PIVOT):
                part = gram_rows[:, row - end : row - end + PIVOT]
                gram[row : row + PIVOT, row:] -= dot_f32(part, gram_rows[:, row - end :], 0, 0)
    norms[...] = jnp.sqrt(left_over / points_total)


def project_out(core, mine, theirs, image, own, points_total):
    size = own.shape[1]
    whole = pl.BlockSpec(memory_space=pltpu.VMEM)
    return pl.pallas_call(
        functools.partial(eliminate, points_total),
        in_specs=[pl.BlockSpec(memory_space=pltpu.SMEM), whole, whole, whole, whole],
        out_specs=(whole, whole),
        out_shape=(
            jax.ShapeDtypeStruct(own.shape, jnp.float32),
            jax.ShapeDtypeStruct((1, size), jnp.float32),
        ),
        scratch_shapes=[
            pltpu.VMEM((size, size), jnp.float32),
            pltpu.VMEM((size, size), jnp.float32),
            pltpu.VMEM(image.shape, jnp.float32),
            pltpu.VMEM((1, size), jnp.float32),
        ],
        compiler_params=pltpu.CompilerParams(vmem_limit_bytes=40 * 2**20),
        name="eliminate",
    )(core[None], mine, theirs, image, own)


def plane_groups():
    return [[2 * chip + core for chip in range(lax.axis_size("col") // 2)] for core in range(2)]


def within_plane(tiles):
    return lax.all_to_all(tiles, "col", 0, 0, axis_index_groups=plane_groups(), tiled=True)


def in_quads(tiles, groups):
    return lax.all_to_all(tiles, "row", 0, 0, axis_index_groups=groups, tiled=True)


def copies(share, count):
    return jnp.broadcast_to(share[None], (count, *share.shape))


def column_sum(share):
    quads = lax.axis_size("row") // 4
    near = [[4 * quad + place for place in range(4)] for quad in range(quads)]
    far = [list(group) for group in zip(*near)]
    rows, columns = share.shape
    parts = jnp.moveaxis(share.reshape(rows, 4, columns // 4), 1, 0)
    part = jnp.sum(in_quads(parts, near), axis=0)
    part = jnp.sum(in_quads(copies(part, quads), far), axis=0)
    return jnp.moveaxis(in_quads(copies(part, 4), near), 0, 1).reshape(rows, columns)


def global_sum(half):
    chips = lax.axis_size("col") // 2
    rows = half.shape[0] // chips
    share = column_sum(jnp.sum(within_plane(half.reshape(chips, rows, -1)), axis=0))
    return within_plane(copies(share, chips)).reshape(half.shape)


def half_of_sums(core, image, own, pair_image, pair_own, own_squares):
    odd = core == 1
    images = jnp.concatenate([image, pair_image], axis=0)
    owns = jnp.concatenate([own, pair_own], axis=0)
    blocks = [images[:, k * 128 : k * 128 + 128] for k in range(4)]
    wide = matmul_hi(jnp.where(odd, blocks[1], blocks[0]), images, 0, 0)
    narrow = matmul_hi(jnp.where(odd, blocks[2], blocks[3]), images[:, 256:], 0, 0)
    gram_part = jnp.where(
        odd,
        jnp.concatenate([wide[:, 128:], narrow], axis=1),
        jnp.concatenate([wide, narrow[:, 128:]], axis=1),
    )
    cross_part = matmul_hi(jnp.where(odd, images[:, 256:], images[:, :256]), owns, 0, 0)
    squares = jnp.pad(own_squares.reshape(4, 128), ((0, 124), (0, 0)))
    return jnp.concatenate([gram_part, cross_part[:128], cross_part[128:], squares], axis=1)


def shards(
    coords, residual_in, link_mask, compress, expand, level_gain, level_couple, partner_perm
):
    rank = compress.shape[1]
    columns = residual_in.shape[1]
    core = lax.axis_index("col") & 1

    gains = [level_gain[0, k * rank : (k + 1) * rank][:, None] for k in range(LEVELS)]
    numbers = jnp.arange(rank, dtype=jnp.int32)[None, :]

    def couple_of(level_at):
        couple = level_couple[:, level_at * rank : (level_at + 1) * rank]
        place = (partner_perm[0, level_at][:, None] == numbers).astype(jnp.float32)
        return matmul_hi(couple, place)

    couples = [couple_of(k) for k in range(LEVELS)]

    by_one = swapped(residual_in, "row", 4)
    by_three = swapped(residual_in, "row", 12)
    compress_two = swapped(compress, "row", 8)
    rows = residual_in.shape[0]
    placed = jnp.pad(coords, ((0, 5), (0, columns - coords.shape[1])))
    near_points = jnp.concatenate([residual_in, placed], axis=0)
    below = from_behind(near_points, ("row", "col"), 1)
    above = from_behind(near_points, ("row", "col"), -1)
    below_rhs, above_rhs = below[:rows], above[:rows]
    below_xyz, above_xyz = below[rows : rows + 3, :rows], above[rows : rows + 3, :rows]

    points = expand.shape[0]
    expand_own = expand * level_gain[:, 4 * rank :]
    from_last = swapped(matmul_hi(expand, couples[4]), "col", 4)

    by_one, compress_two, from_last = lax.optimization_barrier((by_one, compress_two, from_last))
    by_two = swapped(by_one, "row", 12)
    low_map = jnp.concatenate(
        [gains[0] * compress.T, matmul_hi(couples[0], compress_two, 1, 1)], axis=1
    )
    low_map_one = swapped(low_map, "row", 4)
    from_both = swapped(
        matmul_hi(jnp.concatenate([expand_own, from_last], axis=0), couples[3]), "col", 8
    )
    by_two, low_map_one, by_three, from_both = lax.optimization_barrier(
        (by_two, low_map_one, by_three, from_both)
    )

    maps = [expand_own * gains[3][:, 0], from_last * gains[3][:, 0]]
    maps += [from_both[:points], from_both[points:]]
    last_bit, next_bit = (lax.axis_index("col") & 4) > 0, (lax.axis_index("col") & 8) > 0
    maps = [jnp.where(last_bit, maps[k ^ 1], maps[k]) for k in range(4)]
    maps = jnp.concatenate([jnp.where(next_bit, maps[k ^ 2], maps[k]) for k in range(4)], axis=0)

    near_scale = (3.0 * coords.shape[1]) ** (-0.5)
    weights = link_mask.astype(jnp.float32)
    near_field = matmul_hi(kernel_tile(coords, coords), residual_in)
    near_field = near_field + weights[0, 0] * matmul_hi(kernel_tile(coords, below_xyz), below_rhs)
    near_field = near_field + weights[0, 1] * matmul_hi(kernel_tile(coords, above_xyz), above_rhs)
    base = 2.0 * residual_in + near_scale * near_field
    own_squares = jnp.sum(residual_in * residual_in, axis=0)
    pair_own = jnp.where(core == 1, below_rhs, above_rhs)
    pair_squares = jnp.sum(pair_own * pair_own, axis=0)

    coeffs = gains[1] * matmul_hi(low_map, jnp.concatenate([residual_in, by_two], axis=0))
    low_map_one = matmul_hi(couples[1], low_map_one)
    coeffs = coeffs + matmul_hi(low_map_one, jnp.concatenate([by_one, by_three], axis=0))
    coeffs = gains[2] * coeffs + matmul_hi(couples[2], swapped(coeffs, "col", 16))
    given = matmul_hi(maps, coeffs).reshape(4, points, columns)
    quads = [[16 * x + 2 * y + e + 4 * k for k in range(4)] for x in range(2) for y in range(2) for e in range(2)]
    taken = lax.all_to_all(given, "col", 0, 0, axis_index_groups=quads, tiled=True)
    image = base + jnp.sum(taken, axis=0)

    half = half_of_sums(
        core, image, residual_in, swapped(image, "col", 1), pair_own, own_squares + pair_squares
    )
    mine = global_sum(half)
    theirs = swapped(mine, "col", 1)
    points_total = coords.shape[1] * lax.axis_size("row") * lax.axis_size("col")
    new_residual, res_norms = project_out(core, mine, theirs, image, residual_in, points_total)
    return (new_residual, res_norms[0])


def solution(mesh):
    return jax.shard_map(
        shards,
        mesh=mesh,
        in_specs=(
            P(None, ("row", "col")),
            P(("row", "col"), None),
            P(("row", "col"), None),
            P(("row", "col"), None),
            P(("row", "col"), None),
            P(("row", "col"), None),
            P(("row", "col"), None),
            P(("row", "col"), None, None),
        ),
        out_specs=(P(("row", "col"), None), P()),
        check_vma=False,
    )
```

```python
import functools

import jax
import jax.numpy as jnp
from jax import lax
from jax.experimental import pallas as pl
from jax.experimental.pallas import tpu as pltpu
from jax.sharding import PartitionSpec as P

LEVELS = 5


WAVENUM = 6.0
SOFTEN = 0.01
PIVOT = 128
SLAB = 8


def swapped(block, axis, bits):
    return lax.ppermute(block, axis, [(i, i ^ bits) for i in range(lax.axis_size(axis))])


def from_behind(block, axis, distance):
    devices = range(lax.axis_size(axis))
    route = [(i - distance, i) for i in devices if i - distance in devices]
    return lax.ppermute(block, axis, route)


def kernel_tile(own_xyz, other_xyz):
    dist_sq = (own_xyz[0][:, None] - other_xyz[0][None, :]) ** 2
    dist_sq = dist_sq + (own_xyz[1][:, None] - other_xyz[1][None, :]) ** 2
    dist_sq = dist_sq + (own_xyz[2][:, None] - other_xyz[2][None, :]) ** 2
    return jnp.cos(WAVENUM * jnp.sqrt(dist_sq)) / jnp.sqrt(dist_sq + SOFTEN)


def matmul_hi(left, right, left_dim=1, right_dim=0):
    dims = (((left_dim,), (right_dim,)), ((), ()))
    return lax.dot_general(left, right, dims, precision=lax.Precision.HIGHEST)


def three_parts(value):
    high = value.astype(jnp.bfloat16)
    rest = value - high.astype(jnp.float32)
    middle = rest.astype(jnp.bfloat16)
    return high, middle, (rest - middle.astype(jnp.float32)).astype(jnp.bfloat16)


def dot_parts(left, right, left_dim, right_dim):
    def one_pass(first, second, third, fourth):
        return lax.dot_general(
            jnp.concatenate([first, second], axis=left_dim),
            jnp.concatenate([third, fourth], axis=right_dim),
            (((left_dim,), (right_dim,)), ((), ())),
            preferred_element_type=jnp.float32,
        )

    high, middle, low = left if isinstance(left, tuple) else three_parts(left)
    top, mid, last = right if isinstance(right, tuple) else three_parts(right)
    small = one_pass(high, middle, mid, mid) + one_pass(high, low, last, top)
    return one_pass(high, middle, top, top) + small


def self_product(rows, first, count):
    high, middle, low = (part.astype(jnp.float32) for part in three_parts(rows))
    right = jnp.concatenate([high, middle, high, low, high, middle], axis=0)
    left = jnp.concatenate([high, high, middle, high, low, middle], axis=0)[:, first:count]
    return lax.dot_general(
        left.astype(jnp.bfloat16),
        right.astype(jnp.bfloat16),
        (((0,), (0,)), ((), ())),
        preferred_element_type=jnp.float32,
    )


def slab_factor_inverse(slab, at):
    spread = (8, 128)
    block, beside, found = {}, {}, {}
    for i in range(SLAB):
        beside[i, i] = jnp.ones(spread, jnp.float32)
        for j in range(i, SLAB):
            block[i, j] = jnp.broadcast_to(slab[i : i + 1, at + j : at + j + 1], spread)
    for k in range(SLAB):
        pivot = 1.0 / block[k, k]
        for i in range(k + 1, SLAB):
            for j in range(i, SLAB):
                block[i, j] = block[i, j] - (block[k, i] * block[k, j]) * pivot
            ratio = block[k, i] * pivot
            for j in range(k + 1):
                term = ratio * beside[k, j] if j < k else ratio
                beside[i, j] = beside[i, j] - term if (i, j) in beside else -term
    for i in range(SLAB):
        scale = lax.rsqrt(block[i, i])
        for j in range(i + 1):
            found[i, j] = beside[i, j] * scale if j < i else scale
    return found


def sum_of_rows(columns, rows, count):
    left, right = 0.0, 0.0
    for k in range(SLAB):
        left = left + columns[k] * jnp.broadcast_to(rows[k : k + 1, :count], (SLAB, count))
        right = right + columns[k] * jnp.broadcast_to(rows[k : k + 1, count:], (SLAB, count))
    return jnp.concatenate([left, right], axis=1)


def slab_rows(found, slab, count):
    row_at = lax.broadcasted_iota(jnp.int32, (SLAB, count), 0)
    columns = []
    for j in range(SLAB):
        column = jnp.zeros((SLAB, count), jnp.float32)
        for i in range(j, SLAB):
            column = jnp.where(row_at == i, found[i, j], column)
        columns.append(column)
    return sum_of_rows(columns, slab, count)


def after_slab(found, rows, following, at, count):
    held = [jnp.broadcast_to(following[:, at + i : at + i + 1], (SLAB, count)) for i in range(SLAB)]
    columns = []
    for k in range(SLAB):
        columns.append(sum(found[k, i] * held[i] for i in range(k + 1)))
    return following - sum_of_rows(columns, rows, count)


def factor_inverse(block):
    count = block.shape[0]
    row_at = lax.broadcasted_iota(jnp.int32, block.shape, 0)
    col_at = lax.broadcasted_iota(jnp.int32, block.shape, 1)
    rest = jnp.concatenate([block, jnp.where(row_at == col_at, 1.0, 0.0)], axis=1)
    slab, rest = rest[:SLAB], rest[SLAB:]
    done = []
    for at in range(0, count, SLAB):
        found = slab_factor_inverse(slab, at)
        rows = slab_rows(found, slab, count)
        done.append(rows[:, count:])
        if at + SLAB < count:
            slab = after_slab(found, rows, rest[:SLAB], at, count)
        if at + 2 * SLAB < count:
            rest = rest[SLAB:] - self_product(rows, at + 2 * SLAB, count)
    return jnp.concatenate(done, axis=0)


def eliminate(
    points_total, core, mine, theirs, image_in, own_in, new, norms, gram, cross, image, total
):
    size = gram.shape[0]
    image[...] = image_in[...]
    new[...] = own_in[...]

    def unpack(first, second):
        gram[0:128, 0:512] = first[:, 0:512]
        gram[384:512, 384:512] = first[:, 512:640]
        gram[128:256, 128:512] = second[:, 0:384]
        gram[256:384, 256:512] = second[:, 384:640]
        cross[0:128, :] = first[:, 640:1152]
        cross[128:256, :] = first[:, 1152:1664]
        cross[256:384, :] = second[:, 640:1152]
        cross[384:512, :] = second[:, 1152:1664]
        for piece in range(4):
            total[:, piece * 128 : piece * 128 + 128] = first[piece : piece + 1, 1664:1792]

    @pl.when(core[0] == 0)
    def _():
        unpack(mine, theirs)

    @pl.when(core[0] == 1)
    def _():
        unpack(theirs, mine)

    left_over = total[...]
    for at in range(0, size, PIVOT):
        end = at + PIVOT
        inverse = three_parts(factor_inverse(gram[at:end, at:end]))
        cross_rows = dot_parts(inverse, cross[at:end, :], 1, 0)
        left_over = left_over - jnp.sum(cross_rows * cross_rows, axis=0, keepdims=True)
        cross_rows = three_parts(cross_rows)
        image_cols = three_parts(dot_parts(image[:, at:end], inverse, 1, 1))
        new[...] -= dot_parts(image_cols, cross_rows, 1, 0)
        if end < size:
            gram_rows = three_parts(dot_parts(inverse, gram[at:end, end:], 1, 0))
            image[:, end:] -= dot_parts(image_cols, gram_rows, 1, 0)
            cross[end:, :] -= dot_parts(gram_rows, cross_rows, 0, 0)
            for row in range(end, size, PIVOT):
                own = tuple(part[:, row - end : row - end + PIVOT] for part in gram_rows)
                right = tuple(part[:, row - end :] for part in gram_rows)
                gram[row : row + PIVOT, row:] -= dot_parts(own, right, 0, 0)
    norms[...] = jnp.sqrt(left_over / points_total)


def project_out(core, mine, theirs, image, own, points_total):
    size = own.shape[1]
    whole = pl.BlockSpec(memory_space=pltpu.VMEM)
    return pl.pallas_call(
        functools.partial(eliminate, points_total),
        in_specs=[pl.BlockSpec(memory_space=pltpu.SMEM), whole, whole, whole, whole],
        out_specs=(whole, whole),
        out_shape=(
            jax.ShapeDtypeStruct(own.shape, jnp.float32),
            jax.ShapeDtypeStruct((1, size), jnp.float32),
        ),
        scratch_shapes=[
            pltpu.VMEM((size, size), jnp.float32),
            pltpu.VMEM((size, size), jnp.float32),
            pltpu.VMEM(image.shape, jnp.float32),
            pltpu.VMEM((1, size), jnp.float32),
        ],
        compiler_params=pltpu.CompilerParams(vmem_limit_bytes=40 * 2**20),
        name="eliminate",
    )(core[None], mine, theirs, image, own)


def plane_groups():
    return [[2 * chip + core for chip in range(lax.axis_size("col") // 2)] for core in range(2)]


def within_plane(tiles):
    return lax.all_to_all(tiles, "col", 0, 0, axis_index_groups=plane_groups(), tiled=True)


def in_quads(tiles, groups):
    return lax.all_to_all(tiles, "row", 0, 0, axis_index_groups=groups, tiled=True)


def copies(share, count):
    return jnp.broadcast_to(share[None], (count, *share.shape))


def column_sum(share):
    quads = lax.axis_size("row") // 4
    near = [[4 * quad + place for place in range(4)] for quad in range(quads)]
    far = [list(group) for group in zip(*near)]
    rows, columns = share.shape
    parts = jnp.moveaxis(share.reshape(rows, 4, columns // 4), 1, 0)
    part = jnp.sum(in_quads(parts, near), axis=0)
    part = jnp.sum(in_quads(copies(part, quads), far), axis=0)
    return jnp.moveaxis(in_quads(copies(part, 4), near), 0, 1).reshape(rows, columns)


def global_sum(half):
    chips = lax.axis_size("col") // 2
    rows = half.shape[0] // chips
    share = column_sum(jnp.sum(within_plane(half.reshape(chips, rows, -1)), axis=0))
    return within_plane(copies(share, chips)).reshape(half.shape)


def half_of_sums(core, image, own, pair_image, pair_own, own_squares):
    odd = core == 1
    images = jnp.concatenate([image, pair_image], axis=0)
    owns = jnp.concatenate([own, pair_own], axis=0)
    blocks = [images[:, k * 128 : k * 128 + 128] for k in range(4)]
    wide = matmul_hi(jnp.where(odd, blocks[1], blocks[0]), images, 0, 0)
    narrow = matmul_hi(jnp.where(odd, blocks[2], blocks[3]), images[:, 256:], 0, 0)
    gram_part = jnp.where(
        odd,
        jnp.concatenate([wide[:, 128:], narrow], axis=1),
        jnp.concatenate([wide, narrow[:, 128:]], axis=1),
    )
    cross_part = matmul_hi(jnp.where(odd, images[:, 256:], images[:, :256]), owns, 0, 0)
    squares = jnp.pad(own_squares.reshape(4, 128), ((0, 124), (0, 0)))
    return jnp.concatenate([gram_part, cross_part[:128], cross_part[128:], squares], axis=1)


def shards(
    coords, residual_in, link_mask, compress, expand, level_gain, level_couple, partner_perm
):
    rank = compress.shape[1]
    columns = residual_in.shape[1]
    core = lax.axis_index("col") & 1

    gains = [level_gain[0, k * rank : (k + 1) * rank][:, None] for k in range(LEVELS)]
    numbers = jnp.arange(rank, dtype=jnp.int32)[None, :]

    def couple_of(level_at):
        couple = level_couple[:, level_at * rank : (level_at + 1) * rank]
        place = (partner_perm[0, level_at][:, None] == numbers).astype(jnp.float32)
        return matmul_hi(couple, place)

    couples = [couple_of(k) for k in range(LEVELS)]

    by_one = swapped(residual_in, "row", 4)
    by_three = swapped(residual_in, "row", 12)
    compress_two = swapped(compress, "row", 8)
    rows = residual_in.shape[0]
    placed = jnp.pad(coords, ((0, 5), (0, columns - coords.shape[1])))
    near_points = jnp.concatenate([residual_in, placed], axis=0)
    below = from_behind(near_points, ("row", "col"), 1)
    above = from_behind(near_points, ("row", "col"), -1)
    below_rhs, above_rhs = below[:rows], above[:rows]
    below_xyz, above_xyz = below[rows : rows + 3, :rows], above[rows : rows + 3, :rows]

    points = expand.shape[0]
    expand_own = expand * level_gain[:, 4 * rank :]
    from_last = swapped(matmul_hi(expand, couples[4]), "col", 4)

    by_one, compress_two, from_last = lax.optimization_barrier((by_one, compress_two, from_last))
    by_two = swapped(by_one, "row", 12)
    low_map = jnp.concatenate(
        [gains[0] * compress.T, matmul_hi(couples[0], compress_two, 1, 1)], axis=1
    )
    low_map_one = swapped(low_map, "row", 4)
    from_both = swapped(
        matmul_hi(jnp.concatenate([expand_own, from_last], axis=0), couples[3]), "col", 8
    )
    by_two, low_map_one, by_three, from_both = lax.optimization_barrier(
        (by_two, low_map_one, by_three, from_both)
    )

    maps = [expand_own * gains[3][:, 0], from_last * gains[3][:, 0]]
    maps += [from_both[:points], from_both[points:]]
    last_bit, next_bit = (lax.axis_index("col") & 4) > 0, (lax.axis_index("col") & 8) > 0
    maps = [jnp.where(last_bit, maps[k ^ 1], maps[k]) for k in range(4)]
    maps = jnp.concatenate([jnp.where(next_bit, maps[k ^ 2], maps[k]) for k in range(4)], axis=0)

    near_scale = (3.0 * coords.shape[1]) ** (-0.5)
    weights = link_mask.astype(jnp.float32)
    near_field = matmul_hi(kernel_tile(coords, coords), residual_in)
    near_field = near_field + weights[0, 0] * matmul_hi(kernel_tile(coords, below_xyz), below_rhs)
    near_field = near_field + weights[0, 1] * matmul_hi(kernel_tile(coords, above_xyz), above_rhs)
    base = 2.0 * residual_in + near_scale * near_field
    own_squares = jnp.sum(residual_in * residual_in, axis=0)
    pair_own = jnp.where(core == 1, below_rhs, above_rhs)
    pair_squares = jnp.sum(pair_own * pair_own, axis=0)

    coeffs = gains[1] * matmul_hi(low_map, jnp.concatenate([residual_in, by_two], axis=0))
    low_map_one = matmul_hi(couples[1], low_map_one)
    coeffs = coeffs + matmul_hi(low_map_one, jnp.concatenate([by_one, by_three], axis=0))
    coeffs = gains[2] * coeffs + matmul_hi(couples[2], swapped(coeffs, "col", 16))
    given = matmul_hi(maps, coeffs).reshape(4, points, columns)
    quads = [[16 * x + 2 * y + e + 4 * k for k in range(4)] for x in range(2) for y in range(2) for e in range(2)]
    taken = lax.all_to_all(given, "col", 0, 0, axis_index_groups=quads, tiled=True)
    image = base + jnp.sum(taken, axis=0)

    half = half_of_sums(
        core, image, residual_in, swapped(image, "col", 1), pair_own, own_squares + pair_squares
    )
    mine = global_sum(half)
    theirs = swapped(mine, "col", 1)
    points_total = coords.shape[1] * lax.axis_size("row") * lax.axis_size("col")
    new_residual, res_norms = project_out(core, mine, theirs, image, residual_in, points_total)
    return (new_residual, res_norms[0])


def solution(mesh):
    return jax.shard_map(
        shards,
        mesh=mesh,
        in_specs=(
            P(None, ("row", "col")),
            P(("row", "col"), None),
            P(("row", "col"), None),
            P(("row", "col"), None),
            P(("row", "col"), None),
            P(("row", "col"), None),
            P(("row", "col"), None),
            P(("row", "col"), None, None),
        ),
        out_specs=(P(("row", "col"), None), P()),
        check_vma=False,
    )
```

```python
import functools

import jax
import jax.numpy as jnp
from jax import lax
from jax.experimental import pallas as pl
from jax.experimental.pallas import tpu as pltpu
from jax.sharding import PartitionSpec as P

LEVELS = 5


WAVENUM = 6.0
SOFTEN = 0.01
PIVOT = 128
SLAB = 8


def swapped(block, axis, bits):
    return lax.ppermute(block, axis, [(i, i ^ bits) for i in range(lax.axis_size(axis))])


def from_behind(block, axis, distance):
    devices = range(lax.axis_size(axis))
    route = [(i - distance, i) for i in devices if i - distance in devices]
    return lax.ppermute(block, axis, route)


def kernel_tile(own_xyz, other_xyz):
    dist_sq = (own_xyz[0][:, None] - other_xyz[0][None, :]) ** 2
    dist_sq = dist_sq + (own_xyz[1][:, None] - other_xyz[1][None, :]) ** 2
    dist_sq = dist_sq + (own_xyz[2][:, None] - other_xyz[2][None, :]) ** 2
    return jnp.cos(WAVENUM * jnp.sqrt(dist_sq)) / jnp.sqrt(dist_sq + SOFTEN)


def matmul_hi(left, right, left_dim=1, right_dim=0):
    dims = (((left_dim,), (right_dim,)), ((), ()))
    return lax.dot_general(left, right, dims, precision=lax.Precision.HIGHEST)


def three_parts(value):
    high = value.astype(jnp.bfloat16)
    rest = value - high.astype(jnp.float32)
    middle = rest.astype(jnp.bfloat16)
    return high, middle, (rest - middle.astype(jnp.float32)).astype(jnp.bfloat16)


def dot_parts(left, right, left_dim, right_dim):
    def one_pass(first, second, third, fourth):
        return lax.dot_general(
            jnp.concatenate([first, second], axis=left_dim),
            jnp.concatenate([third, fourth], axis=right_dim),
            (((left_dim,), (right_dim,)), ((), ())),
            preferred_element_type=jnp.float32,
        )

    high, middle, low = left if isinstance(left, tuple) else three_parts(left)
    top, mid, last = right if isinstance(right, tuple) else three_parts(right)
    small = one_pass(high, middle, mid, mid) + one_pass(high, low, last, top)
    return one_pass(high, middle, top, top) + small


def self_product(rows, first, count):
    high, middle, low = (part.astype(jnp.float32) for part in three_parts(rows))
    right = jnp.concatenate([high, middle, high, low, high, middle], axis=0)
    left = jnp.concatenate([high, high, middle, high, low, middle], axis=0)[:, first:count]
    return lax.dot_general(
        left.astype(jnp.bfloat16),
        right.astype(jnp.bfloat16),
        (((0,), (0,)), ((), ())),
        preferred_element_type=jnp.float32,
    )


def slab_factor_inverse(slab, at):
    spread = (8, 128)
    block, beside, found = {}, {}, {}
    for i in range(SLAB):
        beside[i, i] = jnp.ones(spread, jnp.float32)
        for j in range(i, SLAB):
            block[i, j] = jnp.broadcast_to(slab[i : i + 1, at + j : at + j + 1], spread)
    for k in range(SLAB):
        pivot = 1.0 / block[k, k]
        for i in range(k + 1, SLAB):
            for j in range(i, SLAB):
                block[i, j] = block[i, j] - (block[k, i] * block[k, j]) * pivot
            ratio = block[k, i] * pivot
            for j in range(k + 1):
                term = ratio * beside[k, j] if j < k else ratio
                beside[i, j] = beside[i, j] - term if (i, j) in beside else -term
    for i in range(SLAB):
        scale = lax.rsqrt(block[i, i])
        for j in range(i + 1):
            found[i, j] = beside[i, j] * scale if j < i else scale
    return found


def sum_of_rows(columns, rows, count):
    left, right = 0.0, 0.0
    for k in range(SLAB):
        left = left + columns[k] * jnp.broadcast_to(rows[k : k + 1, :count], (SLAB, count))
        right = right + columns[k] * jnp.broadcast_to(rows[k : k + 1, count:], (SLAB, count))
    return jnp.concatenate([left, right], axis=1)


def slab_rows(found, slab, count):
    row_at = lax.broadcasted_iota(jnp.int32, (SLAB, count), 0)
    columns = []
    for j in range(SLAB):
        column = jnp.zeros((SLAB, count), jnp.float32)
        for i in range(j, SLAB):
            column = jnp.where(row_at == i, found[i, j], column)
        columns.append(column)
    return sum_of_rows(columns, slab, count)


def after_slab(found, rows, following, at, count):
    held = [jnp.broadcast_to(following[:, at + i : at + i + 1], (SLAB, count)) for i in range(SLAB)]
    columns = []
    for k in range(SLAB):
        columns.append(sum(found[k, i] * held[i] for i in range(k + 1)))
    return following - sum_of_rows(columns, rows, count)


def factor_inverse(block):
    count = block.shape[0]
    row_at = lax.broadcasted_iota(jnp.int32, block.shape, 0)
    col_at = lax.broadcasted_iota(jnp.int32, block.shape, 1)
    rest = jnp.concatenate([block, jnp.where(row_at == col_at, 1.0, 0.0)], axis=1)
    slab, rest = rest[:SLAB], rest[SLAB:]
    done = []
    for at in range(0, count, SLAB):
        found = slab_factor_inverse(slab, at)
        rows = slab_rows(found, slab, count)
        done.append(rows[:, count:])
        if at + SLAB < count:
            slab = after_slab(found, rows, rest[:SLAB], at, count)
        if at + 2 * SLAB < count:
            rest = rest[SLAB:] - self_product(rows, at + 2 * SLAB, count)
    return jnp.concatenate(done, axis=0)


def eliminate(
    points_total, core, mine, theirs, image_in, own_in, new, norms, gram, cross, image, total
):
    size = gram.shape[0]
    image[...] = image_in[...]
    new[...] = own_in[...]

    def unpack(first, second):
        gram[0:128, 0:512] = first[:, 0:512]
        gram[384:512, 384:512] = first[:, 512:640]
        gram[128:256, 128:512] = second[:, 0:384]
        gram[256:384, 256:512] = second[:, 384:640]
        cross[0:128, :] = first[:, 640:1152]
        cross[128:256, :] = first[:, 1152:1664]
        cross[256:384, :] = second[:, 640:1152]
        cross[384:512, :] = second[:, 1152:1664]
        for piece in range(4):
            pair = [first[row : row + 1, 0:64] for row in (120 + 2 * piece, 121 + 2 * piece)]
            total[:, piece * 128 : piece * 128 + 128] = jnp.concatenate(pair, axis=1)

    @pl.when(core[0] == 0)
    def _():
        unpack(mine, theirs)

    @pl.when(core[0] == 1)
    def _():
        unpack(theirs, mine)

    left_over = total[...]
    for at in range(0, size, PIVOT):
        end = at + PIVOT
        inverse = three_parts(factor_inverse(gram[at:end, at:end]))
        cross_rows = dot_parts(inverse, cross[at:end, :], 1, 0)
        left_over = left_over - jnp.sum(cross_rows * cross_rows, axis=0, keepdims=True)
        cross_rows = three_parts(cross_rows)
        image_cols = three_parts(dot_parts(image[:, at:end], inverse, 1, 1))
        new[...] -= dot_parts(image_cols, cross_rows, 1, 0)
        if end < size:
            gram_rows = three_parts(dot_parts(inverse, gram[at:end, end:], 1, 0))
            image[:, end:] -= dot_parts(image_cols, gram_rows, 1, 0)
            cross[end:, :] -= dot_parts(gram_rows, cross_rows, 0, 0)
            for row in range(end, size, PIVOT):
                own = tuple(part[:, row - end : row - end + PIVOT] for part in gram_rows)
                right = tuple(part[:, row - end :] for part in gram_rows)
                gram[row : row + PIVOT, row:] -= dot_parts(own, right, 0, 0)
    norms[...] = jnp.sqrt(left_over / points_total)


def project_out(core, mine, theirs, image, own, points_total):
    size = own.shape[1]
    whole = pl.BlockSpec(memory_space=pltpu.VMEM)
    return pl.pallas_call(
        functools.partial(eliminate, points_total),
        in_specs=[pl.BlockSpec(memory_space=pltpu.SMEM), whole, whole, whole, whole],
        out_specs=(whole, whole),
        out_shape=(
            jax.ShapeDtypeStruct(own.shape, jnp.float32),
            jax.ShapeDtypeStruct((1, size), jnp.float32),
        ),
        scratch_shapes=[
            pltpu.VMEM((size, size), jnp.float32),
            pltpu.VMEM((size, size), jnp.float32),
            pltpu.VMEM(image.shape, jnp.float32),
            pltpu.VMEM((1, size), jnp.float32),
        ],
        compiler_params=pltpu.CompilerParams(vmem_limit_bytes=40 * 2**20),
        name="eliminate",
    )(core[None], mine, theirs, image, own)


def plane_groups():
    return [[2 * chip + core for chip in range(lax.axis_size("col") // 2)] for core in range(2)]


def within_plane(tiles):
    return lax.all_to_all(tiles, "col", 0, 0, axis_index_groups=plane_groups(), tiled=True)


def in_quads(tiles, groups):
    return lax.all_to_all(tiles, "row", 0, 0, axis_index_groups=groups, tiled=True)


def copies(share, count):
    return jnp.broadcast_to(share[None], (count, *share.shape))


def column_sum(share):
    quads = lax.axis_size("row") // 4
    near = [[4 * quad + place for place in range(4)] for quad in range(quads)]
    far = [list(group) for group in zip(*near)]
    rows, columns = share.shape
    parts = jnp.moveaxis(share.reshape(rows, 4, columns // 4), 1, 0)
    part = jnp.sum(in_quads(parts, near), axis=0)
    part = jnp.sum(in_quads(copies(part, quads), far), axis=0)
    return jnp.moveaxis(in_quads(copies(part, 4), near), 0, 1).reshape(rows, columns)


def global_sum(half):
    chips = lax.axis_size("col") // 2
    rows = half.shape[0] // chips
    share = column_sum(jnp.sum(within_plane(half.reshape(chips, rows, -1)), axis=0))
    return within_plane(copies(share, chips)).reshape(half.shape)


def half_of_sums(core, image, own, pair_image, pair_own, own_squares):
    odd = core == 1
    images = jnp.concatenate([image, pair_image], axis=0)
    owns = jnp.concatenate([own, pair_own], axis=0)
    blocks = [images[:, k * 128 : k * 128 + 128] for k in range(4)]
    wide = matmul_hi(jnp.where(odd, blocks[1], blocks[0]), images, 0, 0)
    wide = wide.at[120:, :64].set(own_squares.reshape(8, 64))
    narrow = matmul_hi(jnp.where(odd, blocks[2], blocks[3]), images[:, 256:], 0, 0)
    gram_part = jnp.where(
        odd,
        jnp.concatenate([wide[:, 128:], narrow], axis=1),
        jnp.concatenate([wide, narrow[:, 128:]], axis=1),
    )
    cross_part = matmul_hi(jnp.where(odd, images[:, 256:], images[:, :256]), owns, 0, 0)
    return jnp.concatenate([gram_part, cross_part[:128], cross_part[128:]], axis=1)


def shards(
    coords, residual_in, link_mask, compress, expand, level_gain, level_couple, partner_perm
):
    rank = compress.shape[1]
    columns = residual_in.shape[1]
    core = lax.axis_index("col") & 1

    gains = [level_gain[0, k * rank : (k + 1) * rank][:, None] for k in range(LEVELS)]
    numbers = jnp.arange(rank, dtype=jnp.int32)[None, :]

    def couple_of(level_at):
        couple = level_couple[:, level_at * rank : (level_at + 1) * rank]
        place = (partner_perm[0, level_at][:, None] == numbers).astype(jnp.float32)
        return matmul_hi(couple, place)

    couples = [couple_of(k) for k in range(LEVELS)]

    by_one = swapped(residual_in, "row", 4)
    by_three = swapped(residual_in, "row", 12)
    compress_two = swapped(compress, "row", 8)
    rows = residual_in.shape[0]
    placed = jnp.pad(coords, ((0, 5), (0, columns - coords.shape[1])))
    near_points = jnp.concatenate([residual_in, placed], axis=0)
    below = from_behind(near_points, ("row", "col"), 1)
    above = from_behind(near_points, ("row", "col"), -1)
    below_rhs, above_rhs = below[:rows], above[:rows]
    below_xyz, above_xyz = below[rows : rows + 3, :rows], above[rows : rows + 3, :rows]

    points = expand.shape[0]
    expand_own = expand * level_gain[:, 4 * rank :]
    from_last = swapped(matmul_hi(expand, couples[4]), "col", 4)

    by_one, compress_two, from_last = lax.optimization_barrier((by_one, compress_two, from_last))
    low_map = jnp.concatenate(
        [gains[0] * compress.T, matmul_hi(couples[0], compress_two, 1, 1)], axis=1
    )
    low_map_one = swapped(low_map, "row", 4)
    from_both = swapped(
        matmul_hi(jnp.concatenate([expand_own, from_last], axis=0), couples[3]), "col", 8
    )
    by_two = swapped(by_one, "row", 12)
    by_two, low_map_one, by_three = lax.optimization_barrier((by_two, low_map_one, by_three))

    maps = [expand_own * gains[3][:, 0], from_last * gains[3][:, 0]]
    maps += [from_both[:points], from_both[points:]]
    last_bit, next_bit = (lax.axis_index("col") & 4) > 0, (lax.axis_index("col") & 8) > 0
    maps = [jnp.where(last_bit, maps[k ^ 1], maps[k]) for k in range(4)]
    maps = jnp.concatenate([jnp.where(next_bit, maps[k ^ 2], maps[k]) for k in range(4)], axis=0)

    near_scale = (3.0 * coords.shape[1]) ** (-0.5)
    weights = link_mask.astype(jnp.float32)
    near_field = matmul_hi(kernel_tile(coords, coords), residual_in)
    near_field = near_field + weights[0, 0] * matmul_hi(kernel_tile(coords, below_xyz), below_rhs)
    near_field = near_field + weights[0, 1] * matmul_hi(kernel_tile(coords, above_xyz), above_rhs)
    base = 2.0 * residual_in + near_scale * near_field
    own_squares = jnp.sum(residual_in * residual_in, axis=0)
    pair_own = jnp.where(core == 1, below_rhs, above_rhs)
    pair_squares = jnp.sum(pair_own * pair_own, axis=0)

    coeffs = gains[1] * matmul_hi(low_map, jnp.concatenate([residual_in, by_two], axis=0))
    low_map_one = matmul_hi(couples[1], low_map_one)
    coeffs = coeffs + matmul_hi(low_map_one, jnp.concatenate([by_one, by_three], axis=0))
    coeffs = gains[2] * coeffs + matmul_hi(couples[2], swapped(coeffs, "col", 16))
    given = matmul_hi(maps, coeffs).reshape(4, points, columns)
    quads = [[16 * x + 2 * y + e + 4 * k for k in range(4)] for x in range(2) for y in range(2) for e in range(2)]
    taken = lax.all_to_all(given, "col", 0, 0, axis_index_groups=quads, tiled=True)
    image = base + jnp.sum(taken, axis=0)

    half = half_of_sums(
        core, image, residual_in, swapped(image, "col", 1), pair_own, own_squares + pair_squares
    )
    mine = global_sum(half)
    theirs = swapped(mine, "col", 1)
    points_total = coords.shape[1] * lax.axis_size("row") * lax.axis_size("col")
    new_residual, res_norms = project_out(core, mine, theirs, image, residual_in, points_total)
    return (new_residual, res_norms[0])


def solution(mesh):
    return jax.shard_map(
        shards,
        mesh=mesh,
        in_specs=(
            P(None, ("row", "col")),
            P(("row", "col"), None),
            P(("row", "col"), None),
            P(("row", "col"), None),
            P(("row", "col"), None),
            P(("row", "col"), None),
            P(("row", "col"), None),
            P(("row", "col"), None, None),
        ),
        out_specs=(P(("row", "col"), None), P()),
        check_vma=False,
    )
```

```python
import functools

import jax
import jax.numpy as jnp
from jax import lax
from jax.experimental import pallas as pl
from jax.experimental.pallas import tpu as pltpu
from jax.sharding import PartitionSpec as P

LEVELS = 5


WAVENUM = 6.0
SOFTEN = 0.01
PIVOT = 128
SLAB = 8


def swapped(block, axis, bits):
    return lax.ppermute(block, axis, [(i, i ^ bits) for i in range(lax.axis_size(axis))])


def from_behind(block, axis, distance):
    devices = range(lax.axis_size(axis))
    route = [(i - distance, i) for i in devices if i - distance in devices]
    return lax.ppermute(block, axis, route)


def kernel_tile(own_xyz, other_xyz):
    dist_sq = (own_xyz[0][:, None] - other_xyz[0][None, :]) ** 2
    dist_sq = dist_sq + (own_xyz[1][:, None] - other_xyz[1][None, :]) ** 2
    dist_sq = dist_sq + (own_xyz[2][:, None] - other_xyz[2][None, :]) ** 2
    return jnp.cos(WAVENUM * jnp.sqrt(dist_sq)) / jnp.sqrt(dist_sq + SOFTEN)


def matmul_hi(left, right, left_dim=1, right_dim=0):
    dims = (((left_dim,), (right_dim,)), ((), ()))
    return lax.dot_general(left, right, dims, precision=lax.Precision.HIGHEST)


def three_parts(value):
    high = value.astype(jnp.bfloat16)
    rest = value - high.astype(jnp.float32)
    middle = rest.astype(jnp.bfloat16)
    return high, middle, (rest - middle.astype(jnp.float32)).astype(jnp.bfloat16)


def dot_parts(left, right, left_dim, right_dim):
    def one_pass(first, second, third, fourth):
        return lax.dot_general(
            jnp.concatenate([first, second], axis=left_dim),
            jnp.concatenate([third, fourth], axis=right_dim),
            (((left_dim,), (right_dim,)), ((), ())),
            preferred_element_type=jnp.float32,
        )

    high, middle, low = left if isinstance(left, tuple) else three_parts(left)
    top, mid, last = right if isinstance(right, tuple) else three_parts(right)
    small = one_pass(high, middle, mid, mid) + one_pass(high, low, last, top)
    return one_pass(high, middle, top, top) + small


def self_product(rows, first, count):
    high, middle, low = (part.astype(jnp.float32) for part in three_parts(rows))
    right = jnp.concatenate([high, middle, high, low, high, middle], axis=0)
    left = jnp.concatenate([high, high, middle, high, low, middle], axis=0)[:, first:count]
    return lax.dot_general(
        left.astype(jnp.bfloat16),
        right.astype(jnp.bfloat16),
        (((0,), (0,)), ((), ())),
        preferred_element_type=jnp.float32,
    )


def slab_factor_inverse(slab, at):
    spread = (8, 128)
    block, beside, found = {}, {}, {}
    for i in range(SLAB):
        beside[i, i] = jnp.ones(spread, jnp.float32)
        for j in range(i, SLAB):
            block[i, j] = jnp.broadcast_to(slab[i : i + 1, at + j : at + j + 1], spread)
    for k in range(SLAB):
        pivot = 1.0 / block[k, k]
        for i in range(k + 1, SLAB):
            for j in range(i, SLAB):
                block[i, j] = block[i, j] - (block[k, i] * block[k, j]) * pivot
            ratio = block[k, i] * pivot
            for j in range(k + 1):
                term = ratio * beside[k, j] if j < k else ratio
                beside[i, j] = beside[i, j] - term if (i, j) in beside else -term
    for i in range(SLAB):
        scale = lax.rsqrt(block[i, i])
        for j in range(i + 1):
            found[i, j] = beside[i, j] * scale if j < i else scale
    return found


def sum_of_rows(columns, rows, count):
    left, right = 0.0, 0.0
    for k in range(SLAB):
        left = left + columns[k] * jnp.broadcast_to(rows[k : k + 1, :count], (SLAB, count))
        right = right + columns[k] * jnp.broadcast_to(rows[k : k + 1, count:], (SLAB, count))
    return jnp.concatenate([left, right], axis=1)


def slab_rows(found, slab, count):
    row_at = lax.broadcasted_iota(jnp.int32, (SLAB, count), 0)
    columns = []
    for j in range(SLAB):
        column = jnp.zeros((SLAB, count), jnp.float32)
        for i in range(j, SLAB):
            column = jnp.where(row_at == i, found[i, j], column)
        columns.append(column)
    return sum_of_rows(columns, slab, count)


def after_slab(found, rows, following, at, count):
    held = [jnp.broadcast_to(following[:, at + i : at + i + 1], (SLAB, count)) for i in range(SLAB)]
    columns = []
    for k in range(SLAB):
        columns.append(sum(found[k, i] * held[i] for i in range(k + 1)))
    return following - sum_of_rows(columns, rows, count)


def factor_inverse(block):
    count = block.shape[0]
    row_at = lax.broadcasted_iota(jnp.int32, block.shape, 0)
    col_at = lax.broadcasted_iota(jnp.int32, block.shape, 1)
    rest = jnp.concatenate([block, jnp.where(row_at == col_at, 1.0, 0.0)], axis=1)
    slab, rest = rest[:SLAB], rest[SLAB:]
    done = []
    for at in range(0, count, SLAB):
        found = slab_factor_inverse(slab, at)
        rows = slab_rows(found, slab, count)
        done.append(rows[:, count:])
        if at + SLAB < count:
            slab = after_slab(found, rows, rest[:SLAB], at, count)
        if at + 2 * SLAB < count:
            rest = rest[SLAB:] - self_product(rows, at + 2 * SLAB, count)
    return jnp.concatenate(done, axis=0)


def eliminate(
    points_total, core, mine, theirs, image_in, own_in, new, norms, gram, cross, image, total
):
    size = gram.shape[0]
    image[...] = image_in[...]
    new[...] = own_in[...]

    def unpack(first, second):
        gram[0:128, 0:512] = first[:, 0:512]
        gram[384:512, 384:512] = first[:, 512:640]
        gram[128:256, 128:512] = second[:, 0:384]
        gram[256:384, 256:512] = second[:, 384:640]
        cross[0:128, :] = first[:, 640:1152]
        cross[128:256, :] = first[:, 1152:1664]
        cross[256:384, :] = second[:, 640:1152]
        cross[384:512, :] = second[:, 1152:1664]
        for piece in range(4):
            pair = [first[row : row + 1, 0:64] for row in (120 + 2 * piece, 121 + 2 * piece)]
            total[:, piece * 128 : piece * 128 + 128] = jnp.concatenate(pair, axis=1)

    @pl.when(core[0] == 0)
    def _():
        unpack(mine, theirs)

    @pl.when(core[0] == 1)
    def _():
        unpack(theirs, mine)

    left_over = total[...]
    for at in range(0, size, PIVOT):
        end = at + PIVOT
        inverse = three_parts(factor_inverse(gram[at:end, at:end]))
        cross_rows = dot_parts(inverse, cross[at:end, :], 1, 0)
        left_over = left_over - jnp.sum(cross_rows * cross_rows, axis=0, keepdims=True)
        cross_rows = three_parts(cross_rows)
        image_cols = three_parts(dot_parts(image[:, at:end], inverse, 1, 1))
        new[...] -= dot_parts(image_cols, cross_rows, 1, 0)
        if end < size:
            gram_rows = three_parts(dot_parts(inverse, gram[at:end, end:], 1, 0))
            image[:, end:] -= dot_parts(image_cols, gram_rows, 1, 0)
            cross[end:, :] -= dot_parts(gram_rows, cross_rows, 0, 0)
            for row in range(end, size, PIVOT):
                own = tuple(part[:, row - end : row - end + PIVOT] for part in gram_rows)
                right = tuple(part[:, row - end :] for part in gram_rows)
                gram[row : row + PIVOT, row:] -= dot_parts(own, right, 0, 0)
    norms[...] = jnp.sqrt(left_over / points_total)


def project_out(core, mine, theirs, image, own, points_total):
    size = own.shape[1]
    whole = pl.BlockSpec(memory_space=pltpu.VMEM)
    return pl.pallas_call(
        functools.partial(eliminate, points_total),
        in_specs=[pl.BlockSpec(memory_space=pltpu.SMEM), whole, whole, whole, whole],
        out_specs=(whole, whole),
        out_shape=(
            jax.ShapeDtypeStruct(own.shape, jnp.float32),
            jax.ShapeDtypeStruct((1, size), jnp.float32),
        ),
        scratch_shapes=[
            pltpu.VMEM((size, size), jnp.float32),
            pltpu.VMEM((size, size), jnp.float32),
            pltpu.VMEM(image.shape, jnp.float32),
            pltpu.VMEM((1, size), jnp.float32),
        ],
        compiler_params=pltpu.CompilerParams(vmem_limit_bytes=40 * 2**20),
        name="eliminate",
    )(core[None], mine, theirs, image, own)


def plane_groups():
    return [[2 * chip + core for chip in range(lax.axis_size("col") // 2)] for core in range(2)]


def within_plane(tiles):
    return lax.all_to_all(tiles, "col", 0, 0, axis_index_groups=plane_groups(), tiled=True)


def in_quads(tiles, groups):
    return lax.all_to_all(tiles, "row", 0, 0, axis_index_groups=groups, tiled=True)


def copies(share, count):
    return jnp.broadcast_to(share[None], (count, *share.shape))


def column_sum(share):
    quads = lax.axis_size("row") // 4
    near = [[4 * quad + place for place in range(4)] for quad in range(quads)]
    far = [list(group) for group in zip(*near)]
    rows, columns = share.shape
    parts = jnp.moveaxis(share.reshape(rows, 4, columns // 4), 1, 0)
    part = jnp.sum(in_quads(parts, near), axis=0)
    part = jnp.sum(in_quads(copies(part, quads), far), axis=0)
    return jnp.moveaxis(in_quads(copies(part, 4), near), 0, 1).reshape(rows, columns)


def global_sum(half):
    chips = lax.axis_size("col") // 2
    rows = half.shape[0] // chips
    share = column_sum(jnp.sum(within_plane(half.reshape(chips, rows, -1)), axis=0))
    return within_plane(copies(share, chips)).reshape(half.shape)


def half_of_sums(core, image, own, pair_image, pair_own, own_squares):
    odd = core == 1

    def part(one, other):
        blocks = [one[:, k * 128 : k * 128 + 128] for k in range(4)]
        return (
            matmul_hi(jnp.where(odd, blocks[1], blocks[0]), one, 0, 0),
            matmul_hi(jnp.where(odd, blocks[2], blocks[3]), one[:, 256:], 0, 0),
            matmul_hi(jnp.where(odd, one[:, 256:], one[:, :256]), other, 0, 0),
        )

    parts = zip(part(image, own), part(pair_image, pair_own))
    wide, narrow, cross_part = (first + second for first, second in parts)
    wide = wide.at[120:, :64].set(own_squares.reshape(8, 64))
    gram_part = jnp.where(
        odd,
        jnp.concatenate([wide[:, 128:], narrow], axis=1),
        jnp.concatenate([wide, narrow[:, 128:]], axis=1),
    )
    return jnp.concatenate([gram_part, cross_part[:128], cross_part[128:]], axis=1)


def shards(
    coords, residual_in, link_mask, compress, expand, level_gain, level_couple, partner_perm
):
    rank = compress.shape[1]
    columns = residual_in.shape[1]
    core = lax.axis_index("col") & 1

    gains = [level_gain[0, k * rank : (k + 1) * rank][:, None] for k in range(LEVELS)]
    numbers = jnp.arange(rank, dtype=jnp.int32)[None, :]

    def couple_of(level_at):
        couple = level_couple[:, level_at * rank : (level_at + 1) * rank]
        place = (partner_perm[0, level_at][:, None] == numbers).astype(jnp.float32)
        return matmul_hi(couple, place)

    couples = [couple_of(k) for k in range(LEVELS)]

    by_one = swapped(residual_in, "row", 4)
    by_three = swapped(residual_in, "row", 12)
    compress_two = swapped(compress, "row", 8)
    rows = residual_in.shape[0]
    placed = jnp.pad(coords, ((0, 5), (0, columns - coords.shape[1])))
    near_points = jnp.concatenate([residual_in, placed], axis=0)
    below = from_behind(near_points, ("row", "col"), 1)
    above = from_behind(near_points, ("row", "col"), -1)
    below_rhs, above_rhs = below[:rows], above[:rows]
    below_xyz, above_xyz = below[rows : rows + 3, :rows], above[rows : rows + 3, :rows]

    points = expand.shape[0]
    expand_own = expand * level_gain[:, 4 * rank :]
    from_last = swapped(matmul_hi(expand, couples[4]), "col", 4)

    by_one, compress_two, from_last = lax.optimization_barrier((by_one, compress_two, from_last))
    low_map = jnp.concatenate(
        [gains[0] * compress.T, matmul_hi(couples[0], compress_two, 1, 1)], axis=1
    )
    low_map_one = swapped(low_map, "row", 4)
    from_both = swapped(
        matmul_hi(jnp.concatenate([expand_own, from_last], axis=0), couples[3]), "col", 8
    )
    by_two = swapped(by_one, "row", 12)
    by_two, low_map_one, by_three = lax.optimization_barrier((by_two, low_map_one, by_three))

    maps = [expand_own * gains[3][:, 0], from_last * gains[3][:, 0]]
    maps += [from_both[:points], from_both[points:]]
    last_bit, next_bit = (lax.axis_index("col") & 4) > 0, (lax.axis_index("col") & 8) > 0
    maps = [jnp.where(last_bit, maps[k ^ 1], maps[k]) for k in range(4)]
    maps = jnp.concatenate([jnp.where(next_bit, maps[k ^ 2], maps[k]) for k in range(4)], axis=0)

    near_scale = (3.0 * coords.shape[1]) ** (-0.5)
    weights = link_mask.astype(jnp.float32)
    near_field = matmul_hi(kernel_tile(coords, coords), residual_in)
    near_field = near_field + weights[0, 0] * matmul_hi(kernel_tile(coords, below_xyz), below_rhs)
    near_field = near_field + weights[0, 1] * matmul_hi(kernel_tile(coords, above_xyz), above_rhs)
    base = 2.0 * residual_in + near_scale * near_field
    own_squares = jnp.sum(residual_in * residual_in, axis=0)
    pair_own = jnp.where(core == 1, below_rhs, above_rhs)
    pair_squares = jnp.sum(pair_own * pair_own, axis=0)

    coeffs = gains[1] * matmul_hi(low_map, jnp.concatenate([residual_in, by_two], axis=0))
    low_map_one = matmul_hi(couples[1], low_map_one)
    coeffs = coeffs + matmul_hi(low_map_one, jnp.concatenate([by_one, by_three], axis=0))
    coeffs = gains[2] * coeffs + matmul_hi(couples[2], swapped(coeffs, "col", 16))
    given = matmul_hi(maps, coeffs).reshape(4, points, columns)
    quads = [[16 * x + 2 * y + e + 4 * k for k in range(4)] for x in range(2) for y in range(2) for e in range(2)]
    taken = lax.all_to_all(given, "col", 0, 0, axis_index_groups=quads, tiled=True)
    image = base + jnp.sum(taken, axis=0)

    half = half_of_sums(
        core, image, residual_in, swapped(image, "col", 1), pair_own, own_squares + pair_squares
    )
    mine = global_sum(half)
    theirs = swapped(mine, "col", 1)
    points_total = coords.shape[1] * lax.axis_size("row") * lax.axis_size("col")
    new_residual, res_norms = project_out(core, mine, theirs, image, residual_in, points_total)
    return (new_residual, res_norms[0])


def solution(mesh):
    return jax.shard_map(
        shards,
        mesh=mesh,
        in_specs=(
            P(None, ("row", "col")),
            P(("row", "col"), None),
            P(("row", "col"), None),
            P(("row", "col"), None),
            P(("row", "col"), None),
            P(("row", "col"), None),
            P(("row", "col"), None),
            P(("row", "col"), None, None),
        ),
        out_specs=(P(("row", "col"), None), P()),
        check_vma=False,
    )
```
